32 devices in a mesh: dp: 4 (over y, x), seq: 8 (over z, core).
Axes of the slice: x: 2, y: 2, z: 4, core: 2. Of those that a mesh axis runs over, the one named last changes fastest.
Arguments:
- fine_rows: bfloat16 [4, 8192, 1536], P('dp', 'seq'), may hold values from -6 to 6
- queries: bfloat16 [4, 2048, 1536], P('dp', 'seq'), may hold values from -150 to 150
- value_weight: bfloat16 [1536, 1536], replicated, may hold values from -0.15625 to 0.15625
- block_lists: int32 [4, 32, 4], P('dp'), may hold values from -1 to 63, as said below
- out_grad: bfloat16 [4, 2048, 1536], P('dp', 'seq'), may hold values from -6 to 6
Outputs:
- attended: bfloat16 [4, 2048, 1536], P('dp', 'seq')
- query_grad: bfloat16 [4, 2048, 1536], P('dp', 'seq')
- row_grad: bfloat16 [4, 8192, 1536], P('dp', 'seq')
- weight_grad: float32 [1536, 1536], P('seq')
The draws below stay inside these ranges and needn't reach their ends.
Inputs may be any that keep to these rules, and one draw needn't show every extreme that they name: `block_lists`: entries 0 to 1 of query block j are j * 2 to j * 2 + 1. Entry 2 + m (m from 0 to 1) of a query block on seq index r names one of the 8 blocks held by seq index r - (m + 1) * 2, or is -1 when that index is negative.
All inputs are finite; a program needn't handle non-finite values.
Results may differ from the reference program's by a relative error of at most 0.033.
Values may be sent and summed in bfloat16 or wider, within the bound.
A program may use at most 192 MiB of HBM per device.

```python
import math
import jax
import jax.numpy as jnp
from jax import lax

D = 1536
HEADS = 12
HD = 128
FBLK = 128
QBLK = 64
NSTR = 2
B = 4
LEN = 8192
NC = 2048
NFB = 64
NQB = 32
FB_DEV = 8
QB_DEV = 4
OWN = 2
KB = 4
SDEV = 2


def drawn_pair(key):
    key_rows, key_queries = jax.random.split(key, 2)
    rows = jax.random.truncated_normal(key_rows, -6.0, 6.0, (B, LEN, D), jnp.float32)
    query_rows = jax.random.truncated_normal(key_queries, -6.0, 6.0, (B, NC, D), jnp.float32)
    return (rows, query_rows)


def draw_fine_rows(key, part):
    rows, query_rows = drawn_pair(jax.random.fold_in(key, 7))
    return rows.astype(jnp.bfloat16)


def draw_queries(key, part):
    rows, query_rows = drawn_pair(jax.random.fold_in(key, 7))
    return query_rows.astype(jnp.bfloat16)


def draw_block_lists(key, part):
    blocks = jnp.arange(NQB, dtype=jnp.int32)
    device = blocks // QB_DEV
    own_cols = blocks[:, None] * OWN + jnp.arange(OWN, dtype=jnp.int32)[None, :]
    entries = [jnp.broadcast_to(own_cols[None], (B, NQB, OWN))]
    for far_step in range(NSTR):
        owner = device - (far_step + 1) * SDEV
        pick = jax.random.randint(jax.random.fold_in(key, 100 + far_step), (B, NQB), 0, FB_DEV)
        entry = jnp.where(owner[None, :] >= 0, owner[None, :] * FB_DEV + pick, -1)
        entries.append(entry[..., None])
    return jnp.concatenate(entries, axis=-1).astype(jnp.int32)


def shard_levels(rng, dims, cuts, smallest, high):
    gain = 1.0
    for position, blocks in cuts:
        heights = jax.random.uniform(jax.random.fold_in(jax.random.fold_in(rng, 6), position), (blocks,), jnp.float32, smallest / len(cuts), high / len(cuts))
        gain = gain * jnp.repeat(jnp.exp(heights), dims[position] // blocks).reshape((-1,) + (1,) * (len(dims) - 1 - position))
    return gain


def normal_values(rng, extent, spread, most, cuts=(), kind=jnp.bfloat16):
    values = jax.random.normal(rng, extent, jnp.float32) * spread
    if len(cuts) > 0:
        values = shard_levels(rng, extent, cuts, -0.22, 0.18) * values
    return jnp.clip(values, min=-most, max=most).astype(kind)


def setup_inputs(seed: int = 0) -> dict:
    arg_keys = jax.random.split(jax.random.key(seed), 6)
    return {
        "fine_rows": draw_fine_rows(jax.random.fold_in(arg_keys[5], 71), 0),
        "queries": draw_queries(jax.random.fold_in(arg_keys[5], 71), 0),
        "value_weight": normal_values(arg_keys[2], (D, D), D ** -0.5, 0.15625),
        "block_lists": draw_block_lists(jax.random.fold_in(arg_keys[5], 71), 0),
        "out_grad": normal_values(arg_keys[4], (B, NC, D), 1.0, 6.0, ((0, 4), (1, 8))),
    }


neg_big = -1e+30

def round_low(value):
    return lax.optimization_barrier(value.astype(jnp.bfloat16)).astype(jnp.float32)

def reference(fine_rows, queries, value_weight, block_lists, out_grad):
    score_scale = 1.0 / math.sqrt(HD)

    def one_context(weight_acc, item):
        fine, query, list_rows, out_cot = item
        values = jnp.dot(fine, value_weight, preferred_element_type=jnp.float32).astype(jnp.bfloat16)
        fine_blocks = fine.reshape(NFB, FBLK, D)
        value_blocks = values.reshape(NFB, FBLK, D)

        def one_block(sums, block_item):
            key_sum, value_sum = sums
            query_block, cot_block, list_row = block_item
            is_valid = list_row >= 0
            block_index = jnp.maximum(list_row, 0).astype(jnp.int32)
            key_heads = jnp.take(fine_blocks, block_index, axis=0).reshape(KB * FBLK, HEADS, HD).astype(jnp.float32)
            value_heads = jnp.take(value_blocks, block_index, axis=0).reshape(KB * FBLK, HEADS, HD).astype(jnp.float32)
            query_heads = query_block.reshape(QBLK, HEADS, HD).astype(jnp.float32)
            grad_heads = cot_block.reshape(QBLK, HEADS, HD).astype(jnp.float32)
            scores = jnp.einsum('qhd,khd->hqk', query_heads, key_heads) * score_scale
            col_valid = jnp.repeat(is_valid, FBLK)
            scores = jnp.where(col_valid[None, None, :], scores, neg_big)
            row_top = lax.optimization_barrier(jnp.max(scores, axis=-1, keepdims=True))
            raised = jnp.exp(scores - row_top)
            probs = raised / lax.optimization_barrier(jnp.sum(raised, axis=-1, keepdims=True))
            probs_low = round_low(probs)
            out_low = jnp.einsum('hqk,khd->qhd', probs_low, value_heads).astype(jnp.bfloat16)
            row_delta = lax.optimization_barrier(jnp.sum(grad_heads * out_low.astype(jnp.float32), axis=-1)).T
            dprob = jnp.einsum('qhd,khd->hqk', grad_heads, value_heads)
            dscore = round_low(probs * (dprob - row_delta[..., None]))
            query_part = (jnp.einsum('hqk,khd->qhd', dscore, key_heads) * score_scale).astype(jnp.bfloat16)
            key_part = round_low(jnp.einsum('hqk,qhd->khd', dscore, query_heads) * score_scale).reshape(KB, FBLK, D)
            value_part = round_low(jnp.einsum('hqk,qhd->khd', probs_low, grad_heads)).reshape(KB, FBLK, D)
            key_sum = key_sum.at[block_index].add(key_part)
            value_sum = value_sum.at[block_index].add(value_part)
            return ((key_sum, value_sum), (out_low.reshape(QBLK, D), query_part.reshape(QBLK, D)))
        start_sums = (jnp.zeros((NFB, FBLK, D), jnp.float32), jnp.zeros((NFB, FBLK, D), jnp.float32))
        (key_sum, value_sum), (pooled, query_grads) = lax.scan(one_block, start_sums, (query.reshape(NQB, QBLK, D), out_cot.reshape(NQB, QBLK, D), list_rows))
        value_total = value_sum.reshape(LEN, D).astype(jnp.bfloat16)
        row_grads = (key_sum.reshape(LEN, D) + jnp.dot(value_total, value_weight.T, preferred_element_type=jnp.float32)).astype(jnp.bfloat16)
        weight_acc = weight_acc + jnp.dot(fine.T, value_total, preferred_element_type=jnp.float32)
        return (weight_acc, (pooled.reshape(NC, D), query_grads.reshape(NC, D), row_grads))
    weight_grad, (attended, query_grad, row_grad) = lax.scan(one_context, jnp.zeros((D, D), jnp.float32), (fine_rows, queries, block_lists, out_grad))
    return (attended, query_grad, row_grad, weight_grad)
```

```python
import functools
import math

import jax
import jax.numpy as jnp
from jax import lax
from jax.experimental import pallas as pl
from jax.experimental.pallas import tpu as pltpu
from jax.sharding import PartitionSpec as P

HEADS = 12
FBLK = 128
QBLK = 64
NSTR = 2
DELTA_LANE = 64

neg_big = -1e30


def shifted(block, distance):
    devices = range(lax.axis_size("seq"))
    route = [(i - distance, i) for i in devices if i - distance in devices]
    return lax.ppermute(block, "seq", route)


def rows_by_rows(a, b):
    return lax.dot_general(a, b, (((1,), (1,)), ((), ())), preferred_element_type=jnp.float32)


def turned(a, b):
    return lax.dot_general(a, b, (((0,), (0,)), ((), ())), preferred_element_type=jnp.float32)


def plain(a, b):
    return jnp.dot(a, b, preferred_element_type=jnp.float32)


def head_slices(width):
    size = width // HEADS
    return [slice(h * size, (h + 1) * size) for h in range(HEADS)]


def attend_head(q, k, v, scale):
    scores = rows_by_rows(q, k) * scale
    top = jnp.max(scores, axis=-1, keepdims=True)
    raised = jnp.exp(scores - top)
    total = jnp.sum(raised, axis=-1, keepdims=True)
    out = plain(raised.astype(jnp.bfloat16), v) / total
    return out, top + jnp.log(total)


def merged(out_a, log_a, out_b, log_b):
    top = jnp.maximum(log_a, log_b)
    a = jnp.exp(log_a - top)
    b = jnp.exp(log_b - top)
    total = a + b
    return (out_a * a + out_b * b) / total, top + jnp.log(total)


def lanes(rows):
    return lax.broadcasted_iota(jnp.int32, (rows, 128), 1)


def far_first_kernel(index_ref, q_ref, k_ref, v_ref, out_ref, stat_ref, *, scale):
    lane = lanes(q_ref.shape[0])
    stat = jnp.zeros(stat_ref.shape, jnp.float32)
    for h, cols in enumerate(head_slices(q_ref.shape[1])):
        out, log_total = attend_head(q_ref[:, cols], k_ref[:, cols], v_ref[:, cols], scale)
        out_ref[:, cols] = out.astype(jnp.bfloat16)
        stat = jnp.where(lane == h, log_total, stat)
    stat_ref[...] = stat


def far_merge_kernel(
    index_ref, live_ref, q_ref, k_ref, v_ref, got_ref, got_stat_ref, out_ref, stat_ref, *, scale
):
    live = live_ref[0] > 0
    lane = lanes(q_ref.shape[0])
    stat = jnp.zeros(stat_ref.shape, jnp.float32)
    for h, cols in enumerate(head_slices(q_ref.shape[1])):
        out, log_total = attend_head(q_ref[:, cols], k_ref[:, cols], v_ref[:, cols], scale)
        got_log = jnp.where(live, got_stat_ref[:, h : h + 1], neg_big)
        out, log_total = merged(out, log_total, got_ref[:, cols].astype(jnp.float32), got_log)
        out_ref[:, cols] = out.astype(jnp.bfloat16)
        stat = jnp.where(lane == h, log_total, stat)
    stat_ref[...] = stat


def own_forward_kernel(
    live_ref, q_ref, g_ref, k_ref, v_ref, got_ref, got_stat_ref, out_ref, stat_ref, *, scale
):
    live = live_ref[0] > 0
    lane = lanes(q_ref.shape[0])
    stat = jnp.zeros(stat_ref.shape, jnp.float32)
    for h, cols in enumerate(head_slices(q_ref.shape[1])):
        out, log_total = attend_head(q_ref[:, cols], k_ref[:, cols], v_ref[:, cols], scale)
        got_log = jnp.where(live, got_stat_ref[:, h : h + 1], neg_big)
        out, log_total = merged(out, log_total, got_ref[:, cols].astype(jnp.float32), got_log)
        low = out.astype(jnp.bfloat16)
        out_ref[:, cols] = low
        delta = jnp.sum(
            g_ref[:, cols].astype(jnp.float32) * low.astype(jnp.float32), axis=-1, keepdims=True
        )
        stat = jnp.where(lane == h, log_total, stat)
        stat = jnp.where(lane == DELTA_LANE + h, delta, stat)
    stat_ref[...] = stat


def head_grads(q, g, k, v, log_total, delta, scale):
    probs = jnp.exp(rows_by_rows(q, k) * scale - log_total)
    dscore = (probs * (rows_by_rows(g, v) - delta)).astype(jnp.bfloat16)
    query_part = plain(dscore, k) * scale
    key_part = turned(dscore, q) * scale
    value_part = turned(probs.astype(jnp.bfloat16), g)
    return query_part, key_part, value_part


def own_backward_kernel(
    q_ref, g_ref, k_ref, v_ref, stat_ref, query_ref, key_ref, value_ref, *, scale
):
    for h, cols in enumerate(head_slices(q_ref.shape[1])):
        query_part, key_part, value_part = head_grads(
            q_ref[:, cols],
            g_ref[:, cols],
            k_ref[:, cols],
            v_ref[:, cols],
            stat_ref[:, h : h + 1],
            stat_ref[:, DELTA_LANE + h : DELTA_LANE + h + 1],
            scale,
        )
        query_ref[:, cols] = query_part
        key_ref[:, cols] = key_part.astype(jnp.bfloat16)
        value_ref[:, cols] = value_part.astype(jnp.bfloat16)


def far_backward_kernel(index_ref, *refs, scale, count):
    far = [refs[0:5], refs[5:10]]
    own_key_ref, own_value_ref = refs[10:12]
    query_refs = refs[12:14]
    key_ref, value_ref, key_sum, value_sum = refs[14:18]
    i = pl.program_id(0)

    @pl.when(i == 0)
    def _():
        key_sum[...] = own_key_ref[...].astype(jnp.float32)
        value_sum[...] = own_value_ref[...].astype(jnp.float32)

    for step in range(NSTR):
        q_ref, g_ref, k_ref, v_ref, stat_ref = far[step]
        start = pl.multiple_of(index_ref[step * count + i] * FBLK, FBLK)
        rows = pl.ds(start, FBLK)
        for h, cols in enumerate(head_slices(q_ref.shape[1])):
            query_part, key_part, value_part = head_grads(
                q_ref[:, cols],
                g_ref[:, cols],
                k_ref[:, cols],
                v_ref[:, cols],
                stat_ref[:, h : h + 1],
                stat_ref[:, DELTA_LANE + h : DELTA_LANE + h + 1],
                scale,
            )
            query_refs[step][:, cols] = query_part.astype(jnp.bfloat16)
            key_sum[rows, cols] += key_part
            value_sum[rows, cols] += value_part

    @pl.when(i == pl.num_programs(0) - 1)
    def _():
        key_ref[...] = key_sum[...].astype(jnp.bfloat16)
        value_ref[...] = value_sum[...].astype(jnp.bfloat16)


def params():
    return pltpu.CompilerParams(vmem_limit_bytes=56 * 2**20)


def cost(flops, size):
    return pl.CostEstimate(flops=flops, bytes_accessed=size, transcendentals=0)


def shape(rows, width, kind):
    return jax.ShapeDtypeStruct((rows, width), kind)


def one_context(fine, query, value_weight, list_rows, grad):
    seq_count = lax.axis_size("seq")
    me = lax.axis_index("seq")
    row_count, width = fine.shape
    scale = 1.0 / math.sqrt(width // HEADS)
    fine_count = row_count // FBLK
    query_rows = query.shape[0]
    count = query_rows // QBLK
    own_count = list_rows.shape[1] - NSTR
    own_rows = own_count * FBLK
    stride = seq_count // (NSTR + 1)
    low, full = jnp.bfloat16, jnp.float32

    def served(step):
        peer = lax.dynamic_slice_in_dim(list_rows, (me + (step + 1) * stride) * count, count, 0)
        return jnp.clip(peer[:, own_count + step] - me * fine_count, 0, fine_count - 1)

    index = [served(step) for step in range(NSTR)]
    live = (me >= stride).astype(jnp.int32).reshape(1)

    q1 = shifted(query, -stride)
    values = plain(fine, value_weight).astype(low)
    q2 = shifted(q1, -stride)
    held_grad, q2 = lax.optimization_barrier((grad, q2))
    g1 = shifted(held_grad, -stride)
    g2 = shifted(g1, -stride)

    here = pl.BlockSpec((QBLK, width), lambda i, *_: (i, 0))
    stat_here = pl.BlockSpec((QBLK, 128), lambda i, *_: (i, 0))
    listed = pl.BlockSpec((FBLK, width), lambda i, index, *_: (index[i], 0))
    own = pl.BlockSpec((own_rows, width), lambda i, *_: (i, 0))
    far_flops = 4 * query_rows * FBLK * width
    out_shapes = (shape(query_rows, width, low), shape(query_rows, 128, full))

    o2, s2 = pl.pallas_call(
        functools.partial(far_first_kernel, scale=scale),
        out_shape=out_shapes,
        grid_spec=pltpu.PrefetchScalarGridSpec(
            num_scalar_prefetch=1,
            grid=(count,),
            in_specs=[here, listed, listed],
            out_specs=(here, stat_here),
        ),
        compiler_params=params(),
        cost_estimate=cost(far_flops, 8 * query_rows * width),
        name="far_first",
    )(index[1], q2, fine, values)
    got_o2, got_s2 = shifted(o2, stride), shifted(s2, stride)
    o1, s1 = pl.pallas_call(
        functools.partial(far_merge_kernel, scale=scale),
        out_shape=out_shapes,
        grid_spec=pltpu.PrefetchScalarGridSpec(
            num_scalar_prefetch=2,
            grid=(count,),
            in_specs=[here, listed, listed, here, stat_here],
            out_specs=(here, stat_here),
        ),
        compiler_params=params(),
        cost_estimate=cost(far_flops, 10 * query_rows * width),
        name="far_merge",
    )(index[0], live, q1, fine, values, got_o2, got_s2)
    got_o1, got_s1 = shifted(o1, stride), shifted(s1, stride)
    attended, stat = pl.pallas_call(
        functools.partial(own_forward_kernel, scale=scale),
        out_shape=out_shapes,
        grid_spec=pltpu.PrefetchScalarGridSpec(
            num_scalar_prefetch=1,
            grid=(count,),
            in_specs=[here, here, own, own, here, stat_here],
            out_specs=(here, stat_here),
        ),
        compiler_params=params(),
        cost_estimate=cost(2 * far_flops, 24 * query_rows * width),
        name="own_forward",
    )(live, query, grad, fine, values, got_o1, got_s1)
    stat1 = shifted(stat, -stride)
    stat2 = shifted(stat, -2 * stride)
    own_query, own_key, own_value = pl.pallas_call(
        functools.partial(own_backward_kernel, scale=scale),
        out_shape=(
            shape(query_rows, width, full),
            shape(row_count, width, low),
            shape(row_count, width, low),
        ),
        grid=(count,),
        in_specs=[here, here, own, own, stat_here],
        out_specs=(here, own, own),
        compiler_params=params(),
        cost_estimate=cost(5 * far_flops, 40 * query_rows * width),
        name="own_backward",
    )(query, grad, fine, values, stat)

    def listed_by(step):
        return pl.BlockSpec((FBLK, width), lambda i, index: (index[step * count + i], 0))

    whole = pl.BlockSpec((row_count, width), lambda i, *_: (0, 0), pipeline_mode=pl.Buffered(1))
    far_query1, far_query2, key_sum, value_total = pl.pallas_call(
        functools.partial(far_backward_kernel, scale=scale, count=count),
        out_shape=(
            shape(query_rows, width, low),
            shape(query_rows, width, low),
            shape(row_count, width, low),
            shape(row_count, width, low),
        ),
        grid_spec=pltpu.PrefetchScalarGridSpec(
            num_scalar_prefetch=1,
            grid=(count,),
            in_specs=[here, here, listed_by(0), listed_by(0), stat_here]
            + [here, here, listed_by(1), listed_by(1), stat_here]
            + [whole, whole],
            out_specs=(here, here, whole, whole),
            scratch_shapes=[
                pltpu.VMEM((row_count, width), full),
                pltpu.VMEM((row_count, width), full),
            ],
        ),
        compiler_params=params(),
        cost_estimate=cost(5 * far_flops, 50 * query_rows * width),
        name="far_backward",
    )(
        jnp.concatenate(index),
        q1, g1, fine, values, stat1,
        q2, g2, fine, values, stat2,
        own_key, own_value,
    )
    got_query2 = shifted(far_query2, stride)
    chain = (far_query1.astype(full) + got_query2.astype(full)).astype(low)
    got_query = shifted(chain, stride)
    query_grad = (own_query + got_query.astype(full)).astype(low)
    back_rows = rows_by_rows(value_total, value_weight)
    row_grad = (key_sum.astype(full) + back_rows).astype(low)
    return attended, query_grad, row_grad, value_total


def shards(fine_rows, queries, value_weight, block_lists, out_grad):
    attended, query_grad, row_grad, value_total = one_context(
        fine_rows[0], queries[0], value_weight, block_lists[0], out_grad[0]
    )
    weight_part = turned(fine_rows[0], value_total).astype(jnp.bfloat16)
    weight_share = lax.psum_scatter(weight_part, "seq", scatter_dimension=0, tiled=True)
    weight_grad = lax.psum(weight_share.astype(jnp.float32), "dp")
    return attended[None], query_grad[None], row_grad[None], weight_grad


def solution(mesh):
    return jax.shard_map(
        shards,
        mesh=mesh,
        in_specs=(
            P("dp", "seq", None),
            P("dp", "seq", None),
            P(),
            P("dp", None, None),
            P("dp", "seq", None),
        ),
        out_specs=(
            P("dp", "seq", None),
            P("dp", "seq", None),
            P("dp", "seq", None),
            P("seq", None),
        ),
        check_vma=False,
    )
```

```python
import functools
import math

import jax
import jax.numpy as jnp
from jax import lax
from jax.experimental import pallas as pl
from jax.experimental.pallas import tpu as pltpu
from jax.sharding import PartitionSpec as P

HEADS = 12
FBLK = 128
QBLK = 64
NSTR = 2
DELTA_LANE = 64

neg_big = -1e30


def shifted(block, distance):
    devices = range(lax.axis_size("seq"))
    route = [(i - distance, i) for i in devices if i - distance in devices]
    return lax.ppermute(block, "seq", route)


def rows_by_rows(a, b):
    return lax.dot_general(a, b, (((1,), (1,)), ((), ())), preferred_element_type=jnp.float32)


def turned(a, b):
    return lax.dot_general(a, b, (((0,), (0,)), ((), ())), preferred_element_type=jnp.float32)


def plain(a, b):
    return jnp.dot(a, b, preferred_element_type=jnp.float32)


def head_slices(width):
    size = width // HEADS
    return [slice(h * size, (h + 1) * size) for h in range(HEADS)]


def stacked(parts):
    return jnp.concatenate(parts, axis=0)


def column_of(stat_ref, first):
    return stacked([stat_ref[:, first + h : first + h + 1] for h in range(HEADS)])


def pieces(stack, rows):
    return [stack[h * rows : (h + 1) * rows] for h in range(HEADS)]


def all_scores(a_ref, b_ref):
    return stacked([rows_by_rows(a_ref[:, c], b_ref[:, c]) for c in head_slices(a_ref.shape[1])])


def attend(q_ref, k_ref, v_ref, scale):
    rows, width = q_ref.shape
    scores = all_scores(q_ref, k_ref) * scale
    top = jnp.max(scores, axis=-1, keepdims=True)
    raised = jnp.exp(scores - top)
    total = jnp.sum(raised, axis=-1, keepdims=True)
    low = pieces(raised.astype(jnp.bfloat16), rows)
    out = stacked([plain(low[h], v_ref[:, c]) for h, c in enumerate(head_slices(width))])
    return out, top, total


def write_stat(stat_ref, log_total, delta=None):
    rows = stat_ref.shape[0]
    lane = lax.broadcasted_iota(jnp.int32, stat_ref.shape, 1)
    stat = jnp.zeros(stat_ref.shape, jnp.float32)
    for h, part in enumerate(pieces(log_total, rows)):
        stat = jnp.where(lane == h, part, stat)
    if delta is not None:
        for h, part in enumerate(pieces(delta, rows)):
            stat = jnp.where(lane == DELTA_LANE + h, part, stat)
    stat_ref[...] = stat


def write_out(out_ref, out):
    rows, width = out_ref.shape
    for part, cols in zip(pieces(out, rows), head_slices(width)):
        out_ref[:, cols] = part.astype(out_ref.dtype)


def stack_of(ref):
    return stacked([ref[:, c] for c in head_slices(ref.shape[1])])


def far_first_kernel(index_ref, q_ref, k_ref, v_ref, out_ref, stat_ref, *, scale):
    out, top, total = attend(q_ref, k_ref, v_ref, scale)
    write_out(out_ref, out * (1.0 / total))
    write_stat(stat_ref, top + jnp.log(total))


def attend_and_merge(live_ref, q_ref, k_ref, v_ref, got_ref, got_stat_ref, scale):
    out, top, total = attend(q_ref, k_ref, v_ref, scale)
    got_log = jnp.where(live_ref[0] > 0, column_of(got_stat_ref, 0), neg_big)
    most = jnp.maximum(top, got_log)
    mine = jnp.exp(top - most)
    other = jnp.exp(got_log - most)
    total = total * mine + other
    inverse = 1.0 / total
    out = out * (mine * inverse) + stack_of(got_ref).astype(jnp.float32) * (other * inverse)
    return out, most + jnp.log(total)


def far_merge_kernel(
    index_ref, live_ref, q_ref, k_ref, v_ref, got_ref, got_stat_ref, out_ref, stat_ref, *, scale
):
    out, log_total = attend_and_merge(live_ref, q_ref, k_ref, v_ref, got_ref, got_stat_ref, scale)
    write_out(out_ref, out)
    write_stat(stat_ref, log_total)


def own_forward_kernel(
    live_ref, q_ref, g_ref, k_ref, v_ref, got_ref, got_stat_ref, out_ref, stat_ref, *, scale
):
    out, log_total = attend_and_merge(live_ref, q_ref, k_ref, v_ref, got_ref, got_stat_ref, scale)
    low = out.astype(jnp.bfloat16)
    write_out(out_ref, low)
    delta = jnp.sum(
        stack_of(g_ref).astype(jnp.float32) * low.astype(jnp.float32), axis=-1, keepdims=True
    )
    write_stat(stat_ref, log_total, delta)


def weights_of(q_ref, g_ref, k_ref, v_ref, stat_ref, scale):
    rows = q_ref.shape[0]
    probs = jnp.exp(all_scores(q_ref, k_ref) * scale - column_of(stat_ref, 0))
    dscore = probs * (all_scores(g_ref, v_ref) - column_of(stat_ref, DELTA_LANE))
    return pieces(probs.astype(jnp.bfloat16), rows), pieces(dscore.astype(jnp.bfloat16), rows)


def own_backward_kernel(
    q_ref, g_ref, k_ref, v_ref, stat_ref, query_ref, key_ref, value_ref, *, scale
):
    probs, dscore = weights_of(q_ref, g_ref, k_ref, v_ref, stat_ref, scale)
    for h, cols in enumerate(head_slices(q_ref.shape[1])):
        query_ref[:, cols] = plain(dscore[h], k_ref[:, cols]) * scale
        key_ref[:, cols] = (turned(dscore[h], q_ref[:, cols]) * scale).astype(jnp.bfloat16)
        value_ref[:, cols] = turned(probs[h], g_ref[:, cols]).astype(jnp.bfloat16)


def far_backward_kernel(index_ref, *refs, scale, count):
    far = [refs[0:5], refs[5:10]]
    own_key_ref, own_value_ref = refs[10:12]
    query_refs = refs[12:14]
    key_ref, value_ref, key_sum, value_sum = refs[14:18]
    i = pl.program_id(0)

    @pl.when(i == 0)
    def _():
        key_sum[...] = own_key_ref[...].astype(jnp.float32)
        value_sum[...] = own_value_ref[...].astype(jnp.float32)

    for step in range(NSTR):
        q_ref, g_ref, k_ref, v_ref, stat_ref = far[step]
        start = pl.multiple_of(index_ref[step * count + i] * FBLK, FBLK)
        rows = pl.ds(start, FBLK)
        probs, dscore = weights_of(q_ref, g_ref, k_ref, v_ref, stat_ref, scale)
        for h, cols in enumerate(head_slices(q_ref.shape[1])):
            query_refs[step][:, cols] = (plain(dscore[h], k_ref[:, cols]) * scale).astype(
                jnp.bfloat16
            )
            key_sum[rows, cols] += turned(dscore[h], q_ref[:, cols]) * scale
            value_sum[rows, cols] += turned(probs[h], g_ref[:, cols])

    @pl.when(i == pl.num_programs(0) - 1)
    def _():
        key_ref[...] = key_sum[...].astype(jnp.bfloat16)
        value_ref[...] = value_sum[...].astype(jnp.bfloat16)


PIECES = 3


def bits_of(count):
    return count.bit_length() - 1


def bit(index, k):
    return lax.rem(index // (1 << k), 2)


def plan(p, seq_count, dp_count):
    dp_bits = list(range(bits_of(dp_count)))
    if p % 2:
        dp_bits = dp_bits[::-1]
    seq_bits = list(range(1, bits_of(seq_count)))[::-1]
    return [("seq", 0)] + [("dp", k) for k in dp_bits] + [("seq", k) for k in seq_bits]


def stage_shapes(seq_count, dp_count, rows, width):
    shapes = [(seq_count // 2, rows, width)]
    for axis, _ in plan(0, seq_count, dp_count)[1:]:
        blocks, _, cols = shapes[-1]
        shapes.append((blocks, rows, cols // 2) if axis == "dp" else (blocks // 2, rows, cols))
    return shapes


def sum_kernel(seq_count, dp_count, part_ref, out_ref, *refs):
    stages = 1 + bits_of(dp_count) + bits_of(seq_count) - 1
    got, kept = refs[:stages], refs[stages : 2 * stages - 1]
    gathered, send_sem, recv_sem, gather_send, gather_recv = refs[2 * stages - 1 :]
    rows, width = part_ref.shape[3], part_ref.shape[4]
    cols = width // dp_count
    me = {"seq": lax.axis_index("seq"), "dp": lax.axis_index("dp")}

    def partner(axis, k):
        return {axis: me[axis] + (1 - 2 * bit(me[axis], k)) * (1 << k)}

    def dp_peer(d):
        return {"dp": lax.rem(me["dp"] + d, dp_count)}

    barrier = pltpu.get_barrier_semaphore()
    met = [("seq", k) for k in range(bits_of(seq_count))]
    for axis, k in met:
        pl.semaphore_signal(
            barrier, inc=1, device_id=partner(axis, k), device_id_type=pl.DeviceIdType.MESH
        )
    for d in range(1, dp_count):
        pl.semaphore_signal(
            barrier, inc=1, device_id=dp_peer(d), device_id_type=pl.DeviceIdType.MESH
        )
    pl.semaphore_wait(barrier, len(met) + dp_count - 1)

    def half(ref, p, s, which):
        axis, k = plan(p, seq_count, dp_count)[s]
        if s == 0:
            return ref.at[:, which, p]
        blocks, _, wide = ref.shape[1:]
        if axis == "dp":
            start = pl.multiple_of(which * (wide // 2), wide // 2)
            return ref.at[p, :, :, pl.ds(start, wide // 2)]
        return ref.at[p, pl.ds(which * (blocks // 2), blocks // 2)]

    def source(s):
        return part_ref if s == 0 else kept[s - 1]

    def exchange(p, s):
        axis, k = plan(p, seq_count, dp_count)[s]
        return pltpu.make_async_remote_copy(
            src_ref=half(source(s), p, s, 1 - bit(me[axis], k)),
            dst_ref=got[s].at[p],
            send_sem=send_sem.at[p, s],
            recv_sem=recv_sem.at[p, s],
            device_id=partner(axis, k),
            device_id_type=pl.DeviceIdType.MESH,
        )

    def place(p):
        spot = 0
        for axis, k in plan(p, seq_count, dp_count):
            if axis == "dp":
                spot = 2 * spot + bit(me["dp"], k)
        return spot

    def spread(p, d):
        return pltpu.make_async_remote_copy(
            src_ref=gathered.at[p, place(p)],
            dst_ref=gathered.at[p, place(p)],
            send_sem=gather_send.at[p, d - 1],
            recv_sem=gather_recv.at[p, d - 1],
            device_id=dp_peer(d),
            device_id_type=pl.DeviceIdType.MESH,
        )

    for wave in range(stages + PIECES + 1):
        for p in range(PIECES):
            s = wave - p
            if s < 0 or s > stages + 1:
                continue
            if 0 < s <= stages:
                exchange(p, s - 1).wait_recv()
                axis, k = plan(p, seq_count, dp_count)[s - 1]
                mine = half(source(s - 1), p, s - 1, bit(me[axis], k))
                for b in range(got[s - 1].shape[1]):
                    total = mine[b].astype(jnp.float32) + got[s - 1][p, b].astype(jnp.float32)
                    if s < stages:
                        kept[s - 1][p, b] = total.astype(jnp.bfloat16)
                    else:
                        gathered[p, place(p)] = total.astype(jnp.bfloat16)
            if s < stages:
                exchange(p, s).start()
            elif s == stages:
                for d in range(1, dp_count):
                    spread(p, d).start()
            else:
                for d in range(1, dp_count):
                    spread(p, d).wait_recv()
                for c in range(dp_count):
                    out_ref[p * rows : (p + 1) * rows, c * cols : (c + 1) * cols] = gathered[
                        p, c
                    ].astype(jnp.float32)
    for p in range(PIECES):
        for s in range(stages):
            exchange(p, s).wait_send()
        for d in range(1, dp_count):
            spread(p, d).wait_send()


def summed(part):
    seq_count, dp_count = lax.axis_size("seq"), lax.axis_size("dp")
    height, width = part.shape
    share = height // seq_count
    rows = share // PIECES
    shapes = stage_shapes(seq_count, dp_count, rows, width)
    low, dma = jnp.bfloat16, pltpu.SemaphoreType.DMA
    return pl.pallas_call(
        functools.partial(sum_kernel, seq_count, dp_count),
        out_shape=shape(share, width, jnp.float32),
        in_specs=[pl.BlockSpec(memory_space=pltpu.VMEM)],
        out_specs=pl.BlockSpec(memory_space=pltpu.VMEM),
        scratch_shapes=[pltpu.VMEM((PIECES, *s), low) for s in shapes]
        + [pltpu.VMEM((PIECES, *s), low) for s in shapes[:-1]]
        + [
            pltpu.VMEM((PIECES, dp_count, rows, width // dp_count), low),
            dma((PIECES, len(shapes))),
            dma((PIECES, len(shapes))),
            dma((PIECES, dp_count - 1)),
            dma((PIECES, dp_count - 1)),
        ],
        compiler_params=pltpu.CompilerParams(
            collective_id=0, has_side_effects=True, vmem_limit_bytes=40 * 2**20
        ),
        name="weight_sum",
    )(part.reshape(seq_count // 2, 2, PIECES, rows, width))


def params():
    return pltpu.CompilerParams(vmem_limit_bytes=56 * 2**20)


def cost(flops, size):
    return pl.CostEstimate(flops=flops, bytes_accessed=size, transcendentals=0)


def shape(rows, width, kind):
    return jax.ShapeDtypeStruct((rows, width), kind)


def one_context(fine, query, value_weight, list_rows, grad):
    seq_count = lax.axis_size("seq")
    me = lax.axis_index("seq")
    row_count, width = fine.shape
    scale = 1.0 / math.sqrt(width // HEADS)
    fine_count = row_count // FBLK
    query_rows = query.shape[0]
    count = query_rows // QBLK
    own_count = list_rows.shape[1] - NSTR
    own_rows = own_count * FBLK
    stride = seq_count // (NSTR + 1)
    low, full = jnp.bfloat16, jnp.float32

    def served(step):
        peer = lax.dynamic_slice_in_dim(list_rows, (me + (step + 1) * stride) * count, count, 0)
        return jnp.clip(peer[:, own_count + step] - me * fine_count, 0, fine_count - 1)

    index = [served(step) for step in range(NSTR)]
    live = (me >= stride).astype(jnp.int32).reshape(1)

    q1 = shifted(query, -stride)
    values = plain(fine, value_weight).astype(low)
    q2 = shifted(q1, -stride)
    held_grad, q2 = lax.optimization_barrier((grad, q2))
    g1 = shifted(held_grad, -stride)
    g2 = shifted(g1, -stride)

    here = pl.BlockSpec((QBLK, width), lambda i, *_: (i, 0))
    stat_here = pl.BlockSpec((QBLK, 128), lambda i, *_: (i, 0))
    listed = pl.BlockSpec((FBLK, width), lambda i, index, *_: (index[i], 0))
    own = pl.BlockSpec((own_rows, width), lambda i, *_: (i, 0))
    far_flops = 4 * query_rows * FBLK * width
    out_shapes = (shape(query_rows, width, low), shape(query_rows, 128, full))

    o2, s2 = pl.pallas_call(
        functools.partial(far_first_kernel, scale=scale),
        out_shape=out_shapes,
        grid_spec=pltpu.PrefetchScalarGridSpec(
            num_scalar_prefetch=1,
            grid=(count,),
            in_specs=[here, listed, listed],
            out_specs=(here, stat_here),
        ),
        compiler_params=params(),
        cost_estimate=cost(far_flops, 8 * query_rows * width),
        name="far_first",
    )(index[1], q2, fine, values)
    got_o2, got_s2 = shifted(o2, stride), shifted(s2, stride)
    o1, s1 = pl.pallas_call(
        functools.partial(far_merge_kernel, scale=scale),
        out_shape=out_shapes,
        grid_spec=pltpu.PrefetchScalarGridSpec(
            num_scalar_prefetch=2,
            grid=(count,),
            in_specs=[here, listed, listed, here, stat_here],
            out_specs=(here, stat_here),
        ),
        compiler_params=params(),
        cost_estimate=cost(far_flops, 10 * query_rows * width),
        name="far_merge",
    )(index[0], live, q1, fine, values, got_o2, got_s2)
    got_o1, got_s1 = shifted(o1, stride), shifted(s1, stride)
    attended, stat = pl.pallas_call(
        functools.partial(own_forward_kernel, scale=scale),
        out_shape=out_shapes,
        grid_spec=pltpu.PrefetchScalarGridSpec(
            num_scalar_prefetch=1,
            grid=(count,),
            in_specs=[here, here, own, own, here, stat_here],
            out_specs=(here, stat_here),
        ),
        compiler_params=params(),
        cost_estimate=cost(2 * far_flops, 24 * query_rows * width),
        name="own_forward",
    )(live, query, grad, fine, values, got_o1, got_s1)
    stat1 = shifted(stat, -stride)
    stat2 = shifted(stat, -2 * stride)
    own_query, own_key, own_value = pl.pallas_call(
        functools.partial(own_backward_kernel, scale=scale),
        out_shape=(
            shape(query_rows, width, full),
            shape(row_count, width, low),
            shape(row_count, width, low),
        ),
        grid=(count,),
        in_specs=[here, here, own, own, stat_here],
        out_specs=(here, own, own),
        compiler_params=params(),
        cost_estimate=cost(5 * far_flops, 40 * query_rows * width),
        name="own_backward",
    )(query, grad, fine, values, stat)

    def listed_by(step):
        return pl.BlockSpec((FBLK, width), lambda i, index: (index[step * count + i], 0))

    whole = pl.BlockSpec((row_count, width), lambda i, *_: (0, 0), pipeline_mode=pl.Buffered(1))
    far_query1, far_query2, key_sum, value_total = pl.pallas_call(
        functools.partial(far_backward_kernel, scale=scale, count=count),
        out_shape=(
            shape(query_rows, width, low),
            shape(query_rows, width, low),
            shape(row_count, width, low),
            shape(row_count, width, low),
        ),
        grid_spec=pltpu.PrefetchScalarGridSpec(
            num_scalar_prefetch=1,
            grid=(count,),
            in_specs=[here, here, listed_by(0), listed_by(0), stat_here]
            + [here, here, listed_by(1), listed_by(1), stat_here]
            + [whole, whole],
            out_specs=(here, here, whole, whole),
            scratch_shapes=[
                pltpu.VMEM((row_count, width), full),
                pltpu.VMEM((row_count, width), full),
            ],
        ),
        compiler_params=params(),
        cost_estimate=cost(5 * far_flops, 50 * query_rows * width),
        name="far_backward",
    )(
        jnp.concatenate(index),
        q1, g1, fine, values, stat1,
        q2, g2, fine, values, stat2,
        own_key, own_value,
    )
    got_query2 = shifted(far_query2, stride)
    chain = (far_query1.astype(full) + got_query2.astype(full)).astype(low)
    weight_part = turned(fine, value_total).astype(low)
    back_rows = rows_by_rows(value_total, value_weight)
    row_grad = (key_sum.astype(full) + back_rows).astype(low)
    chain, weight_part, row_grad = lax.optimization_barrier((chain, weight_part, row_grad))
    got_query = shifted(chain, stride)
    weight_grad = summed(weight_part)
    query_grad = (own_query + got_query.astype(full)).astype(low)
    return attended, query_grad, row_grad, weight_grad


def shards(fine_rows, queries, value_weight, block_lists, out_grad):
    attended, query_grad, row_grad, weight_grad = one_context(
        fine_rows[0], queries[0], value_weight, block_lists[0], out_grad[0]
    )
    return attended[None], query_grad[None], row_grad[None], weight_grad


def solution(mesh):
    return jax.shard_map(
        shards,
        mesh=mesh,
        in_specs=(
            P("dp", "seq", None),
            P("dp", "seq", None),
            P(),
            P("dp", None, None),
            P("dp", "seq", None),
        ),
        out_specs=(
            P("dp", "seq", None),
            P("dp", "seq", None),
            P("dp", "seq", None),
            P("seq", None),
        ),
        check_vma=False,
    )
```
